128 devices in a mesh: dom: 32 (over x, z, core), grp: 4 (over y).
Axes of the slice: x: 4, y: 4, z: 4, core: 2. Of those that a mesh axis runs over, the one named last changes fastest.
Arguments:
- x_current: bfloat16 [524288, 128], P(('dom', 'grp')), may hold values from -6 to 6
- x_cached: bfloat16 [524288, 128], P(('dom', 'grp')), may hold values from -6 to 6
- w_self: bfloat16 [128, 512], replicated, may hold values from -0.5 to 0.5
- w_neigh: bfloat16 [128, 512], replicated, may hold values from -1 to 1
- bias: float32 [512], replicated, may hold values from -3 to 3
- tile_columns: int32 [4096, 40], P(('dom', 'grp')), may hold values from 0 to 255
- tile_count: int32 [4096], P(('dom', 'grp')), may hold values from 1 to 40, as said below
- adjacency: int32 [4096, 40, 2048], P(('dom', 'grp')), may hold values from 0 to 255, as said below
- degree: int32 [524288], P(('dom', 'grp')), may hold values from 1 to 5128, as said below
- boundary_blocks: int32 [128, 1], P(('dom', 'grp')), may hold values from 0 to 31
Outputs:
- hidden: bfloat16 [524288, 512], P(('dom', 'grp'))
The draws below stay inside these ranges and needn't reach their ends.
Inputs may be any that keep to these rules, and one draw needn't show every extreme that they name: `tile_count`: every device has a row block with all 40 slots live. `adjacency`: 8 entries of a tile row packed into each word, bit b for column 8 c + b. `degree`: at least the number of ones in the row of the live tiles of the node's row block.
All inputs are finite; a program needn't handle non-finite values.
Results may differ from the reference program's by a relative error of at most 0.0025.
Values may be sent and summed in bfloat16 or wider, within the bound.
A program may use at most 192 MiB of HBM per device.

```python
import jax
import jax.numpy as jnp
from jax import lax

F = 128
H = 512
TILE = 128
TPR = 40
BB = 1
NODES = 524288
DBLK = 32
PBLK = 128
ROWBLOCKS = 4096
N_DOM = 32
N_GRP = 4


def count_bits(words):
    value = words - (lax.shift_right_logical(words, 1) & 1431655765)
    value = (value & 858993459) + (lax.shift_right_logical(value, 2) & 858993459)
    value = value + lax.shift_right_logical(value, 4) & 252645135
    return lax.shift_right_logical(value * 16843009, 24)


def tile_tables(key):
    folded = jax.random.fold_in(key, 11)
    keys = jax.random.split(folded, 6)
    blocks = jnp.arange(ROWBLOCKS, dtype=jnp.int32)
    base_draw = jax.random.randint(keys[0], (ROWBLOCKS,), 0, TPR, dtype=jnp.int32)
    heaviness = jax.random.randint(keys[1], (N_DOM,), 2, 7, dtype=jnp.int32)
    counts = jnp.minimum(TPR, 1 + base_draw * heaviness[blocks // PBLK] // 4)
    picked = jax.random.randint(keys[2], (N_DOM * N_GRP,), 0, DBLK, dtype=jnp.int32)
    filled = blocks % DBLK == picked[blocks // DBLK]
    counts = jnp.where(filled, TPR, counts).astype(jnp.int32)
    shape = (ROWBLOCKS, TPR, TILE * TILE // 8)
    packed = jax.random.randint(keys[3], shape, 0, 256, dtype=jnp.int32)
    for layer in range(4):
        packed = packed & jax.random.randint(jax.random.fold_in(keys[4], layer), shape, 0, 256, dtype=jnp.int32)
    packed = packed.at[0, 0, 0].set(255).at[0, 0, 1].set(0)
    ones = count_bits(packed).reshape(ROWBLOCKS, TPR, TILE, TILE // 8).sum(-1)
    live_mask = (jnp.arange(TPR, dtype=jnp.int32)[None, :] < counts[:, None]).astype(jnp.int32)
    row_ones = (ones * live_mask[:, :, None]).sum(1).reshape(-1)
    degree = row_ones + jax.random.randint(keys[5], (NODES,), 1, 9, dtype=jnp.int32)
    degree = degree.at[0].set(TPR * TILE + 8)
    return (counts, packed, degree.astype(jnp.int32))


def draw_tile_count(key, part):
    return tile_tables(key)[0]


def draw_adjacency(key, part):
    return tile_tables(key)[1]


def draw_degree(key, part):
    return tile_tables(key)[2]


def plant(result, stream_key, least, largest):
    extent = result.shape
    index_at = [jax.random.randint(jax.random.fold_in(stream_key, axis), (), 0, extent[axis]) for axis in range(len(extent))]
    result = result.at[tuple(index_at)].set(least)
    longest = extent.index(max(extent))
    index_at[longest] = (index_at[longest] + 1) % extent[longest]
    return result.at[tuple(index_at)].set(largest)


def block_scale(key, shape, cuts, smallest, high):
    def one(axis_at, shards_of):
        heights = jax.random.uniform(jax.random.fold_in(jax.random.fold_in(key, 6), axis_at), (shards_of,), jnp.float32, smallest / len(cuts), high / len(cuts))
        return jnp.repeat(jnp.exp(heights), shape[axis_at] // shards_of).reshape((-1,) + (1,) * (len(shape) - axis_at - 1))

    factor_of = one(*cuts[0])
    for cut in cuts[1:]:
        factor_of = factor_of * one(*cut)
    return factor_of


def scatter_about(own_key, shape, spread, limit, cuts=(), kind=jnp.bfloat16):
    factor_of = block_scale(own_key, shape, cuts, -0.22, 0.18) if cuts else 1.0
    drawn = jax.random.normal(own_key, shape, jnp.float32) * spread * factor_of
    return jnp.minimum(jnp.maximum(drawn, -limit), limit).astype(kind)


def setup_inputs(seed: int = 0) -> dict:
    key_list = jax.random.split(jax.random.key(seed), 11)
    return {
        "x_current": scatter_about(key_list[0], (NODES, F), 1.0, 6.0, ((0, 128),)),
        "x_cached": scatter_about(key_list[1], (NODES, F), 1.0, 6.0, ((0, 128),)),
        "w_self": scatter_about(key_list[2], (F, H), F ** -0.5, 0.5),
        "w_neigh": scatter_about(key_list[3], (F, H), (F // 4) ** -0.5, 1.0),
        "bias": scatter_about(key_list[4], (H,), 0.5, 3.0, (), jnp.float32),
        "tile_columns": plant(jax.random.randint(key_list[5], (ROWBLOCKS, TPR), 0, PBLK + N_DOM * N_GRP * BB), jax.random.fold_in(key_list[5], 1), 0, (PBLK + N_DOM * N_GRP * BB) - 1).astype(jnp.int32),
        "tile_count": draw_tile_count(jax.random.fold_in(key_list[10], 71), 0),
        "adjacency": draw_adjacency(jax.random.fold_in(key_list[10], 71), 0),
        "degree": draw_degree(jax.random.fold_in(key_list[10], 71), 0),
        "boundary_blocks": plant(jax.random.randint(key_list[9], (N_DOM * N_GRP, BB), 0, DBLK), jax.random.fold_in(key_list[9], 1), 0, DBLK - 1).astype(jnp.int32),
    }


def block_sums(block_table, columns, counts, packed, rowblock_ids):
    group_size = columns.shape[0]
    shifts = jnp.arange(8, dtype=jnp.int32)
    bit_values = (packed.reshape(group_size, TPR, TILE, TILE // 8, 1) >> shifts) & 1
    live_mask = (jnp.arange(TPR, dtype=jnp.int32)[None, :] < counts[:, None]).astype(jnp.int32)
    adjacent = (bit_values.reshape(group_size, TPR, TILE, TILE) * live_mask[:, :, None, None]).astype(jnp.float32)
    partition = rowblock_ids // PBLK
    index_rows = jnp.where(columns < PBLK, partition[:, None] * PBLK + columns, ROWBLOCKS + columns - PBLK).astype(jnp.int32)
    gathered = block_table[index_rows].astype(jnp.float32)
    return jnp.einsum("stij,stjf->sif", adjacent, gathered)


def reference(x_current, x_cached, w_self, w_neigh, bias, tile_columns, tile_count, adjacency, degree, boundary_blocks):
    devices = N_DOM * N_GRP
    cached_blocks = x_cached.reshape(ROWBLOCKS, TILE, F)
    device_base = jnp.arange(devices, dtype=jnp.int32) * DBLK
    halo_blocks = cached_blocks[(device_base[:, None] + boundary_blocks).reshape(-1).astype(jnp.int32)]
    block_table = jnp.concatenate([x_current.reshape(ROWBLOCKS, TILE, F), halo_blocks], axis=0)
    group_size = 16 if ROWBLOCKS % 16 == 0 else 1
    turns = ROWBLOCKS // group_size
    rowblock_ids = jnp.arange(ROWBLOCKS, dtype=jnp.int32).reshape(turns, group_size)

    def one_group(pieces):
        return block_sums(block_table, pieces[0], pieces[1], pieces[2], pieces[3])

    totals = lax.map(one_group, (tile_columns.reshape(turns, group_size, TPR), tile_count.reshape(turns, group_size), adjacency.reshape(turns, group_size, TPR, -1), rowblock_ids))
    totals = totals.reshape(NODES, F)
    average = (totals / degree.astype(jnp.float32)[:, None]).astype(jnp.bfloat16)
    summed = jnp.dot(x_current, w_self, preferred_element_type=jnp.float32) + jnp.dot(average, w_neigh, preferred_element_type=jnp.float32) + bias
    return jnp.maximum(summed, 0.0).astype(jnp.bfloat16)
```

```python
import jax
import jax.numpy as jnp
from jax import lax
from jax.experimental import pallas as pl
from jax.experimental.pallas import tpu as pltpu
from jax.sharding import PartitionSpec as P

MESH = pl.DeviceIdType.MESH
SIDE = 4
BLOCK = 128
RB = 32
SLOTS = 40
WORDS = 640
ROWS = RB * BLOCK
FAN = 16
CHUNK = 4
CHUNKS = RB // CHUNK


def gather_kernel(xcur, chosen, part, halo, local_sem, send_sem, recv_sem):
    dom = lax.axis_index("dom")
    y = lax.axis_index("grp")
    core = dom % 2
    z = (dom // 2) % SIDE
    x = dom // (2 * SIDE)

    def at(xx, zz, cc, yy):
        return ((xx * SIDE + zz) * 2 + cc, yy)

    up, down, far = (y + 1) % SIDE, (y + 3) % SIDE, (y + 2) % SIDE
    y_up, y_down, y_far = at(x, z, core, up), at(x, z, core, down), at(x, z, core, far)
    x_up, x_down = at((x + 1) % SIDE, z, core, y), at((x + 3) % SIDE, z, core, y)
    z_up, z_down = at(x, (z + 1) % SIDE, core, y), at(x, (z + 3) % SIDE, core, y)
    sibling = at(x, z, 1 - core, y)
    peers = [y_up, y_down, y_far, x_up, x_down, z_up, z_down, sibling]
    barrier = pltpu.get_barrier_semaphore()
    for peer in peers:
        pl.semaphore_signal(barrier, inc=1, device_id=peer, device_id_type=MESH)
    pl.semaphore_wait(barrier, len(peers))

    started = []

    def send(src, dst, sem, to):
        copy = pltpu.make_async_remote_copy(
            src_ref=src,
            dst_ref=dst,
            send_sem=send_sem.at[sem],
            recv_sem=recv_sem.at[sem],
            device_id=to,
            device_id_type=MESH,
        )
        copy.start()
        started.append(copy)

    def landed(dst, sem):
        pltpu.make_async_remote_copy(
            src_ref=dst,
            dst_ref=dst,
            send_sem=send_sem.at[sem],
            recv_sem=recv_sem.at[sem],
            device_id=sibling,
            device_id_type=MESH,
        ).wait_recv()

    def blocks(first, count):
        return halo.at[pl.ds(pl.multiple_of(first * BLOCK, BLOCK), count * BLOCK)]

    def rows(first, count):
        return part.at[pl.ds(pl.multiple_of(first, BLOCK), count)]

    base = core * 64

    def place(yy):
        ring = jnp.where(yy < 2, z * SIDE + x, x * SIDE + z)
        return base + (yy // 2) * 32 + ring * 2 + yy % 2

    own = blocks(place(y), 1)
    own_part = rows(y * ROWS, ROWS)
    block_copy = pltpu.make_async_copy(chosen, own, local_sem.at[0])
    block_copy.start()
    for sem, peer in enumerate((y_up, y_down, y_far)):
        send(chosen, own, sem, peer)
    send(xcur, own_part, 3, y_up)
    send(xcur, own_part, 4, y_down)
    part_copy = pltpu.make_async_copy(xcur, own_part, local_sem.at[1])
    part_copy.start()
    block_copy.wait()
    landed(blocks(place(down), 1), 0)
    landed(blocks(place(up), 1), 1)
    landed(blocks(place(far), 1), 2)

    first = [
        (lambda m: base + (z * SIDE + m) * 2, x, x_up, x_down),
        (lambda m: base + 32 + (x * SIDE + m) * 2, z, z_up, z_down),
    ]
    second = [
        (lambda m: base + m * 8, z, z_up, z_down),
        (lambda m: base + 32 + m * 8, x, x_up, x_down),
    ]
    for half, (piece, me, pos, neg) in enumerate(first):
        sem = 8 + 4 * half
        send(blocks(piece(me), 2), blocks(piece(me), 2), sem, pos)
        send(blocks(piece(me), 2), blocks(piece(me), 2), sem + 1, neg)
    for half, (piece, me, pos, neg) in enumerate(first):
        sem = 8 + 4 * half
        low, high = piece((me + 3) % SIDE), piece((me + 1) % SIDE)
        landed(blocks(low, 2), sem)
        send(blocks(low, 1), blocks(low, 1), sem + 2, pos)
        landed(blocks(high, 2), sem + 1)
        send(blocks(high + 1, 1), blocks(high + 1, 1), sem + 3, neg)
    for half, (piece, me, _, _) in enumerate(first):
        sem = 8 + 4 * half
        opposite = piece((me + 2) % SIDE)
        landed(blocks(opposite, 1), sem + 2)
        landed(blocks(opposite + 1, 1), sem + 3)
        piece2, me2, pos2, neg2 = second[half]
        mine = blocks(piece2(me2), 8)
        send(mine, mine, 16 + 4 * half, pos2)
        send(mine, mine, 17 + 4 * half, neg2)
        send(mine, mine, 24 + 5 * half, sibling)
    for half, (piece, me, pos, neg) in enumerate(second):
        sem = 16 + 4 * half
        low, high = piece((me + 3) % SIDE), piece((me + 1) % SIDE)
        landed(blocks(low, 8), sem)
        send(blocks(low, 4), blocks(low, 4), sem + 2, pos)
        send(blocks(low, 8), blocks(low, 8), 25 + 5 * half, sibling)
        landed(blocks(high, 8), sem + 1)
        send(blocks(high + 4, 4), blocks(high + 4, 4), sem + 3, neg)
        send(blocks(high, 8), blocks(high, 8), 26 + 5 * half, sibling)
    part_half = ROWS // 2
    landed(rows(down * ROWS, ROWS), 3)
    send(rows(down * ROWS, part_half), rows(down * ROWS, part_half), 5, y_up)
    landed(rows(up * ROWS, ROWS), 4)
    send(rows(up * ROWS + part_half, part_half), rows(up * ROWS + part_half, part_half), 6, y_down)
    for half, (piece, me, _, _) in enumerate(second):
        sem = 16 + 4 * half
        opposite = piece((me + 2) % SIDE)
        landed(blocks(opposite, 4), sem + 2)
        send(blocks(opposite, 4), blocks(opposite, 4), 27 + 5 * half, sibling)
        landed(blocks(opposite + 4, 4), sem + 3)
        send(blocks(opposite + 4, 4), blocks(opposite + 4, 4), 28 + 5 * half, sibling)
    other = (1 - core) * 64
    for half, (start, me) in enumerate(((other, z), (other + 32, x))):
        sem = 24 + 5 * half
        landed(blocks(start + me * 8, 8), sem)
        landed(blocks(start + (me + 3) % SIDE * 8, 8), sem + 1)
        landed(blocks(start + (me + 1) % SIDE * 8, 8), sem + 2)
        landed(blocks(start + (me + 2) % SIDE * 8, 4), sem + 3)
        landed(blocks(start + (me + 2) % SIDE * 8 + 4, 4), sem + 4)
    part_copy.wait()
    landed(rows(far * ROWS, part_half), 5)
    landed(rows(far * ROWS + part_half, part_half), 6)
    for copy in started:
        copy.wait_send()


def gather(xcur, chosen):
    hbm = pl.BlockSpec(memory_space=pl.ANY)
    return pl.pallas_call(
        gather_kernel,
        out_shape=(
            jax.ShapeDtypeStruct((SIDE * ROWS, BLOCK), jnp.bfloat16),
            jax.ShapeDtypeStruct((128 * BLOCK, BLOCK), jnp.bfloat16),
        ),
        in_specs=[hbm, hbm],
        out_specs=(hbm, hbm),
        scratch_shapes=[
            pltpu.SemaphoreType.DMA((2,)),
            pltpu.SemaphoreType.DMA((34,)),
            pltpu.SemaphoreType.DMA((34,)),
        ],
        compiler_params=pltpu.CompilerParams(collective_id=0, has_side_effects=True),
        name="gather",
    )(xcur, chosen)


def layer_kernel(
    cols, counts, words_hbm, part_hbm, halo_hbm, xown_hbm, w, bias, degree, out_hbm,
    groups, words, table, xown, totals, out, turned, word_sem, table_sem, out_sem,
):
    def word_copy(c):
        span = pl.ds(c * CHUNK * WORDS, CHUNK * WORDS)
        return pltpu.make_async_copy(words_hbm.at[span], words.at[span], word_sem.at[c])

    def out_copy(c):
        span = pl.ds(pl.multiple_of(c * CHUNK * BLOCK, BLOCK), CHUNK * BLOCK)
        return pltpu.make_async_copy(out.at[span], out_hbm.at[span], out_sem.at[c])

    part_copy = pltpu.make_async_copy(part_hbm, table.at[pl.ds(0, SIDE * ROWS)], table_sem.at[0])
    halo_copy = pltpu.make_async_copy(halo_hbm, table.at[pl.ds(SIDE * ROWS, 128 * BLOCK)], table_sem.at[1])
    own_copy = pltpu.make_async_copy(xown_hbm, xown, table_sem.at[2])
    for copy in (part_copy, halo_copy, own_copy):
        copy.start()
    for c in range(CHUNKS):
        word_copy(c).start()

    def list_groups(r, at):
        def one(q, at):
            groups[at] = r * 16 + q
            return at + 1

        return lax.fori_loop(0, (counts[r] + 3) // 4, one, at)

    total = lax.fori_loop(0, RB, list_groups, 0)
    for k in range(FAN):
        groups[total + k] = -1
    totals[...] = jnp.zeros_like(totals)
    for copy in (part_copy, halo_copy, own_copy):
        copy.wait()
    for c in range(CHUNKS):
        word_copy(c).wait()

    lane = lax.broadcasted_iota(jnp.int32, (16, BLOCK), 1)
    source = lane // 8
    bit = lane % 8
    low_bit = (1 << bit).astype(jnp.int16)
    high_bit = jnp.where(bit == 7, -32768, 1 << (bit + 8)).astype(jnp.int16)
    one = jnp.ones((16, BLOCK), jnp.bfloat16)
    zero = jnp.zeros((16, BLOCK), jnp.bfloat16)

    def product(at):
        code = groups[at]
        live = code >= 0
        code = jnp.maximum(code, 0)
        r = code // 16
        q = code % 16
        n = jnp.where(live, counts[r], 0)
        first = r * WORDS + (q // 2) * BLOCK + (q % 2) * 4
        packed, features = None, []
        for k in range(4):
            t = q * 4 + k
            keep = jnp.where(t < n, 255 << (8 * k) if k < 3 else -16777216, 0).astype(jnp.int32)
            word = (words[pl.ds(first + k, 16, stride=8), :] << (8 * k)) & keep
            packed = word if packed is None else packed | word
            features.append(table[pl.ds(pl.multiple_of(cols[r, t] * BLOCK, BLOCK), BLOCK), :])
        tiles = [[], [], [], []]
        for m in range(8):
            spread = jnp.take_along_axis(packed, source + 16 * m, axis=1, mode="promise_in_bounds")
            low = spread.astype(jnp.int16)
            high = (spread >> 16).astype(jnp.int16)
            for tile, half, mask in zip(tiles, (low, low, high, high), (low_bit, high_bit) * 2):
                tile.append(jnp.where((half & mask) != 0, one, zero))
        adjacent = jnp.concatenate([jnp.concatenate(tile, axis=0) for tile in tiles], axis=1)
        return r, jnp.dot(adjacent, jnp.concatenate(features, axis=0), preferred_element_type=jnp.float32)

    @pl.loop(0, (total + FAN - 1) // FAN)
    def _(step):
        for r, value in [product(step * FAN + k) for k in range(FAN)]:
            totals[pl.ds(pl.multiple_of(r * BLOCK, BLOCK), BLOCK), :] += value

    @pl.loop(0, CHUNKS)
    def _(c):
        for k in range(CHUNK):
            r = c * CHUNK + k
            span = pl.ds(pl.multiple_of(r * BLOCK, BLOCK), BLOCK)
            for m in range(8):
                turned[k, pl.ds(m, 16, stride=8), :] = totals[pl.ds(r * BLOCK + m * 16, 16), :]
            row = degree[r // 8, pl.ds(r % 8, 1), :].astype(jnp.float32)
            divisor = jnp.broadcast_to(row, (BLOCK, BLOCK)).T
            average = (turned[k] / divisor).astype(jnp.bfloat16)
            both = jnp.concatenate([xown[span, :], average], axis=1)
            hidden = jnp.dot(both, w[...], preferred_element_type=jnp.float32) + bias[...]
            out[span, :] = jnp.maximum(hidden, 0.0).astype(jnp.bfloat16)
        out_copy(c).start()

    for c in range(CHUNKS):
        out_copy(c).wait()


def layer(cols, counts, adjacency, part, halo, xown, w_self, w_neigh, bias, degree):
    words = adjacency.reshape(RB, 5, 8, 16, BLOCK).transpose(0, 1, 3, 2, 4).reshape(RB * WORDS, BLOCK)
    vmem = pl.BlockSpec(memory_space=pltpu.VMEM)
    smem = pl.BlockSpec(memory_space=pltpu.SMEM)
    hbm = pl.BlockSpec(memory_space=pl.ANY)
    return pl.pallas_call(
        layer_kernel,
        out_shape=jax.ShapeDtypeStruct((ROWS, 512), jnp.bfloat16),
        in_specs=[smem, smem, hbm, hbm, hbm, hbm, vmem, vmem, vmem],
        out_specs=hbm,
        scratch_shapes=[
            pltpu.SMEM((352,), jnp.int32),
            pltpu.VMEM((RB * WORDS, BLOCK), jnp.int32),
            pltpu.VMEM((256 * BLOCK, BLOCK), jnp.bfloat16),
            pltpu.VMEM((ROWS, BLOCK), jnp.bfloat16),
            pltpu.VMEM((ROWS, BLOCK), jnp.float32),
            pltpu.VMEM((ROWS, 512), jnp.bfloat16),
            pltpu.VMEM((CHUNK, BLOCK, BLOCK), jnp.float32),
            pltpu.SemaphoreType.DMA((CHUNKS,)),
            pltpu.SemaphoreType.DMA((3,)),
            pltpu.SemaphoreType.DMA((CHUNKS,)),
        ],
        compiler_params=pltpu.CompilerParams(vmem_limit_bytes=56 * 2**20),
        name="layer",
    )(
        cols, counts, words, part, halo, xown, jnp.concatenate([w_self, w_neigh], axis=0),
        bias.reshape(1, 512), degree.reshape(SIDE, 8, BLOCK),
    )


def table_index(columns):
    e = columns - 128
    y, core, z, x = e % 4, e // 4 % 2, e // 8 % 4, e // 32
    place = core * 64 + (y // 2) * 32 + jnp.where(y < 2, z * 4 + x, x * 4 + z) * 2 + y % 2
    return jnp.where(columns < 128, columns, 128 + place)


def on_device(
    x_current, x_cached, w_self, w_neigh, bias, tile_columns, tile_count, adjacency, degree, boundary_blocks
):
    chosen = lax.dynamic_slice(x_cached, (boundary_blocks[0, 0] * BLOCK, 0), (BLOCK, BLOCK))
    part, halo = gather(x_current, chosen)
    cols = table_index(tile_columns)
    return layer(cols, tile_count, adjacency, part, halo, x_current, w_self, w_neigh, bias, degree)


def solution(mesh):
    rows = P(("dom", "grp"), None)
    line = P(("dom", "grp"))
    return jax.shard_map(
        on_device,
        mesh=mesh,
        in_specs=(rows, rows, P(), P(), P(), rows, line, P(("dom", "grp"), None, None), line, rows),
        out_specs=rows,
        check_vma=False,
    )
```

```python
import jax
import jax.numpy as jnp
from jax import lax
from jax.experimental import pallas as pl
from jax.experimental.pallas import tpu as pltpu
from jax.sharding import PartitionSpec as P

MESH = pl.DeviceIdType.MESH
SIDE = 4
BLOCK = 128
RB = 32
SLOTS = 40
WORDS = 640
ROWS = RB * BLOCK
NEAR = 12
HALO = 20
REST = 64
WHO, LEFT = 126, 127
FAN = 8
CHUNK = 4
CHUNKS = RB // CHUNK


def sort_slots(cols, counts, me, wide, live):
    wide[...] = jnp.zeros_like(wide)
    wide[:, :SLOTS] = cols[...]
    for r in range(RB):
        live[pl.ds(r, 1), :] = jnp.full((1, BLOCK), counts[r], jnp.int32)
    c = wide[...]
    t = lax.broadcasted_iota(jnp.int32, (RB, BLOCK), 1)
    on = t < live[...]
    far = (((c >> 5) - me) & 3) == 2
    kind = jnp.where(on, jnp.where(c < 128, jnp.where(far, 2, 0), 1), 3)
    e = c - 128
    y, core, z, x = e & 3, (e >> 2) & 1, (e >> 3) & 3, (e >> 5) & 3
    place = core * 64 + (y >> 1) * 32 + jnp.where(y < 2, z * 4 + x, x * 4 + z) * 2 + (y & 1)
    index = jnp.where(c < 128, c, 128 + place)
    entry = t | (index << 10) | (1 << 18)
    both = (kind << 19) | entry
    table = jnp.zeros((RB, BLOCK), jnp.int32)
    nears = halos = rests = jnp.zeros((RB, BLOCK), jnp.int32)
    for s in range(SLOTS):
        one = jnp.broadcast_to(both[:, s : s + 1], (RB, BLOCK))
        kind = one >> 19
        near = (kind == 0) & (nears < NEAR)
        halo = (kind == 1) & (halos < HALO)
        rest = (kind < 3) & jnp.logical_not(near | halo)
        target = jnp.where(near, nears, jnp.where(halo, NEAR + halos, jnp.where(rest, REST + rests, -1)))
        table = jnp.where(target == t, one & ((1 << 19) - 1), table)
        nears += jnp.where(near, 1, 0)
        halos += jnp.where(halo, 1, 0)
        rests += jnp.where(rest, 1, 0)
    table = jnp.where(t == LEFT, rests, jnp.where(t == WHO, me, table))
    return table


class Unpack:
    def __init__(self):
        lane = lax.broadcasted_iota(jnp.int32, (16, BLOCK), 1)
        self.source = lane >> 3
        bit = lane & 7
        self.low_bit = (1 << bit).astype(jnp.int16)
        self.high_bit = jnp.where(bit == 7, -32768, 1 << (bit + 8)).astype(jnp.int16)

    def four(self, words, rows, keeps):
        one = jnp.ones((16, BLOCK), jnp.bfloat16)
        zero = jnp.zeros((16, BLOCK), jnp.bfloat16)
        packed = None
        for k, (row, keep) in enumerate(zip(rows, keeps)):
            mask = keep & (255 << (8 * k) if k < 3 else -16777216)
            word = (words[row] << (8 * k)) & mask
            packed = word if packed is None else packed | word
        tiles = [[], [], [], []]
        for m in range(8):
            spread = jnp.take_along_axis(packed, self.source + 16 * m, axis=1, mode="promise_in_bounds")
            low = spread.astype(jnp.int16)
            high = (spread >> 16).astype(jnp.int16)
            for tile, half, mask in zip(tiles, (low, low, high, high), (self.low_bit, self.high_bit) * 2):
                tile.append(jnp.where((half & mask) != 0, one, zero))
        return [jnp.concatenate(tile, axis=0) for tile in tiles]


def sum_tiles(unpack, plan, r, first, count, words, table, blocks):
    tiles, features = [], []
    for group in range(count // 4):
        entries = [plan[r, first + group * 4 + k] for k in range(4)]
        rows = [r * SLOTS + (e & 1023) for e in entries]
        tiles += unpack.four(words, rows, [-(e >> 18) for e in entries])
        for e in entries:
            block = (e >> 10) & (blocks - 1)
            features.append(table[block])
    return jnp.dot(
        jnp.concatenate(tiles, axis=1), jnp.concatenate(features, axis=0), preferred_element_type=jnp.float32
    )


def gather_kernel(
    cols_hbm, counts_hbm, exported, degree_hbm, xcur, cached_hbm, words_hbm,
    plan, words, table, totals, divisor,
    cols, counts, degree, wide, live, cached, raw, part, halo, local_sem, send_sem, recv_sem,
):
    dom = lax.axis_index("dom")
    y = lax.axis_index("grp")
    core = dom % 2
    z = (dom // 2) % SIDE
    x = dom // (2 * SIDE)

    def at(xx, zz, cc, yy):
        return ((xx * SIDE + zz) * 2 + cc, yy)

    up, down, far = (y + 1) % SIDE, (y + 3) % SIDE, (y + 2) % SIDE
    y_up, y_down, y_far = at(x, z, core, up), at(x, z, core, down), at(x, z, core, far)
    x_others = [at((x + k) % SIDE, z, core, y) for k in (3, 1, 2)]
    z_others = [at(x, (z + k) % SIDE, core, y) for k in (3, 1, 2)]
    sibling = at(x, z, 1 - core, y)
    cached_copy = pltpu.make_async_copy(cached_hbm, cached, local_sem.at[0])
    cached_copy.start()
    words_copy = pltpu.make_async_copy(words_hbm, raw, local_sem.at[2])
    words_copy.start()
    small_copies = [
        pltpu.make_async_copy(src, dst, local_sem.at[7 + k])
        for k, (src, dst) in enumerate(
            ((cols_hbm, cols), (counts_hbm, counts), (degree_hbm, degree))
        )
    ]
    for copy in small_copies:
        copy.start()
    peers = [y_up, y_down, y_far, *x_others, *z_others, sibling]
    barrier = pltpu.get_barrier_semaphore()
    for peer in peers:
        pl.semaphore_signal(barrier, inc=1, device_id=peer, device_id_type=MESH)
    pl.semaphore_wait(barrier, len(peers))

    started = []

    def send(src, dst, sem, to):
        copy = pltpu.make_async_remote_copy(
            src_ref=src,
            dst_ref=dst,
            send_sem=send_sem.at[sem],
            recv_sem=recv_sem.at[sem],
            device_id=to,
            device_id_type=MESH,
        )
        copy.start()
        started.append(copy)

    def landed(dst, sem):
        pltpu.make_async_remote_copy(
            src_ref=dst,
            dst_ref=dst,
            send_sem=send_sem.at[sem],
            recv_sem=recv_sem.at[sem],
            device_id=sibling,
            device_id_type=MESH,
        ).wait_recv()

    def blocks(first, count):
        return halo.at[pl.ds(first, count)]

    def rows(first, count):
        return part.at[pl.ds(first, count)]

    def far_rows(first):
        return table.at[pl.ds(first, RB // 2)]

    base = core * 64

    def place(yy):
        ring = jnp.where(yy < 2, z * SIDE + x, x * SIDE + z)
        return base + (yy // 2) * 32 + ring * 2 + yy % 2

    own = blocks(place(y), 1)
    own_part = rows(y * RB, RB)
    cached_copy.wait()
    for copy in small_copies:
        copy.wait()
    chosen = cached[exported[0, 0]]
    halo[place(y)] = chosen
    for sem, peer in enumerate((y_up, y_down, y_far)):
        send(own, own, sem, peer)
    send(xcur, own_part, 3, y_up)
    send(xcur, own_part, 4, y_down)
    part_copy = pltpu.make_async_copy(xcur, own_part, local_sem.at[1])
    part_copy.start()
    wide[...] = sort_slots(cols, counts, y, wide, live)
    plan_copy = pltpu.make_async_copy(wide, plan, local_sem.at[0])
    plan_copy.start()
    landed(blocks(place(down), 1), 0)
    landed(blocks(place(up), 1), 1)
    landed(blocks(place(far), 1), 2)

    first = [
        (lambda m: base + (z * SIDE + m) * 2, x, x_others),
        (lambda m: base + 32 + (x * SIDE + m) * 2, z, z_others),
    ]
    second = [
        (lambda m: base + m * 8, z, z_others),
        (lambda m: base + 32 + m * 8, x, x_others),
    ]
    for half, (piece, me, others) in enumerate(first):
        for k, other in enumerate(others):
            send(blocks(piece(me), 2), blocks(piece(me), 2), 8 + 4 * half + k, other)

    words_copy.wait()

    @pl.loop(0, RB)
    def _(r):
        for t in range(SLOTS):
            slot = raw[pl.ds(r * WORDS + (t // 8) * BLOCK + t % 8, 16, stride=8), :]
            words[r * SLOTS + t] = slot

    for half, (piece, me, _) in enumerate(first):
        for k, d in enumerate((1, 3, 2)):
            landed(blocks(piece((me + d) % SIDE), 2), 8 + 4 * half + k)
        piece2, me2, others2 = second[half]
        mine = blocks(piece2(me2), 8)
        for k in (2, 0, 1):
            send(mine, mine, 16 + 4 * half + k, others2[k])
        send(mine, mine, 24 + 4 * half, sibling)

    @pl.loop(0, RB)
    def _(r):
        row = degree[r // 8, pl.ds(r % 8, 1), :].astype(jnp.float32)
        divisor[pl.ds(pl.multiple_of(r * BLOCK, BLOCK), BLOCK), :] = jnp.broadcast_to(row, (BLOCK, BLOCK)).T

    def pass_on(k, d):
        for half, (piece, me, _) in enumerate(second):
            got = blocks(piece((me + d) % SIDE), 8)
            landed(got, 16 + 4 * half + k)
            send(got, got, 25 + 4 * half + k, sibling)

    pass_on(0, 1)
    pass_on(1, 3)
    part_half = RB // 2
    landed(rows(down * RB, RB), 3)
    send(rows(down * RB, part_half), far_rows(down * RB), 5, y_up)
    landed(rows(up * RB, RB), 4)
    send(rows(up * RB + part_half, part_half), far_rows(up * RB + part_half), 6, y_down)
    pass_on(2, 2)
    part_copy.wait()
    plan_copy.wait()
    unpack = Unpack()

    @pl.loop(0, RB // 4)
    def _(step):
        for k in range(4):
            r = step * 4 + k
            value = sum_tiles(unpack, plan, r, 0, NEAR, words, part, 128)
            totals[pl.ds(pl.multiple_of(r * BLOCK, BLOCK), BLOCK), :] = value

    other = (1 - core) * 64
    for half, (start, me) in enumerate(((other, z), (other + 32, x))):
        for k, d in enumerate((0, 1, 3, 2)):
            landed(blocks(start + (me + d) % SIDE * 8, 8), 24 + 4 * half + k)
    near_copies = [
        pltpu.make_async_copy(rows(n * RB, RB), table.at[pl.ds(n * RB, RB)], local_sem.at[3 + k])
        for k, n in enumerate((y, up, down))
    ]
    near_copies.append(pltpu.make_async_copy(halo, table.at[pl.ds(SIDE * RB, 128)], local_sem.at[6]))
    for copy in near_copies:
        copy.start()

    @pl.loop(0, RB // 2)
    def _(step):
        for k in range(2):
            r = step * 2 + k
            value = sum_tiles(unpack, plan, r, NEAR, HALO, words, halo, 128)
            totals[pl.ds(pl.multiple_of(r * BLOCK, BLOCK), BLOCK), :] += value

    for copy in near_copies:
        copy.wait()
    landed(far_rows(far * RB), 5)
    landed(far_rows(far * RB + part_half), 6)
    for copy in started:
        copy.wait_send()


def gather(cols, counts, exported, degree, xcur, cached, words):
    hbm = pl.BlockSpec(memory_space=pl.ANY)
    vmem = pl.BlockSpec(memory_space=pltpu.VMEM)
    smem = pl.BlockSpec(memory_space=pltpu.SMEM)
    operands = [
        pltpu.with_memory_space_constraint(a, pltpu.HBM) for a in (cols, counts, degree, xcur, cached, words)
    ]
    operands.insert(2, exported)
    return pl.pallas_call(
        gather_kernel,
        out_shape=(
            pltpu.SMEM((RB, BLOCK), jnp.int32),
            pltpu.VMEM((RB * SLOTS, 16, BLOCK), jnp.int32),
            pltpu.VMEM((256, BLOCK, BLOCK), jnp.bfloat16),
            pltpu.VMEM((ROWS, BLOCK), jnp.float32),
            pltpu.VMEM((ROWS, BLOCK), jnp.float32),
        ),
        in_specs=[hbm, hbm, smem, hbm, hbm, hbm, hbm],
        out_specs=(smem, vmem, vmem, vmem, vmem),
        scratch_shapes=[
            pltpu.VMEM((RB, SLOTS), jnp.int32),
            pltpu.SMEM((RB,), jnp.int32),
            pltpu.VMEM((SIDE, 8, BLOCK), jnp.int32),
            pltpu.VMEM((RB, BLOCK), jnp.int32),
            pltpu.VMEM((RB, BLOCK), jnp.int32),
            pltpu.VMEM((RB, BLOCK, BLOCK), jnp.bfloat16),
            pltpu.VMEM((RB * WORDS, BLOCK), jnp.int32),
            pltpu.VMEM((SIDE * RB, BLOCK, BLOCK), jnp.bfloat16),
            pltpu.VMEM((128, BLOCK, BLOCK), jnp.bfloat16),
            pltpu.SemaphoreType.DMA((11,)),
            pltpu.SemaphoreType.DMA((32,)),
            pltpu.SemaphoreType.DMA((32,)),
        ],
        compiler_params=pltpu.CompilerParams(
            collective_id=0, has_side_effects=True, vmem_limit_bytes=26 * 2**20
        ),
        name="gather",
    )(*operands)


def layer_kernel(
    plan, words, table, before, divisor, w_self, w_neigh, bias, out_hbm, groups, totals, out, turned, out_sem
):
    def out_copy(c):
        span = pl.ds(pl.multiple_of(c * CHUNK * BLOCK, BLOCK), CHUNK * BLOCK)
        return pltpu.make_async_copy(out.at[span], out_hbm.at[span], out_sem.at[c])

    def list_groups(r, at):
        def one(q, at):
            groups[at] = r * 16 + q
            return at + 1

        return lax.fori_loop(0, (plan[r, LEFT] + 3) // 4, one, at)

    total = lax.fori_loop(0, RB, list_groups, 0)
    for k in range(FAN):
        groups[total + k] = -1
    totals[...] = before[...]
    unpack = Unpack()

    def product(at):
        code = groups[at]
        live = code >= 0
        code = jnp.maximum(code, 0)
        r = code >> 4
        first = jnp.where(live, REST + (code & 15) * 4, BLOCK - 8)
        return r, sum_tiles(unpack, plan, r, first, 4, words, table, 256)

    @pl.loop(0, (total + FAN - 1) // FAN)
    def _(step):
        for r, value in [product(step * FAN + k) for k in range(FAN)]:
            totals[pl.ds(pl.multiple_of(r * BLOCK, BLOCK), BLOCK), :] += value

    mine = plan[0, WHO] * RB

    @pl.loop(0, CHUNKS)
    def _(c):
        spans = [pl.ds(pl.multiple_of((c * CHUNK + k) * BLOCK, BLOCK), BLOCK) for k in range(CHUNK)]
        for k in range(CHUNK):
            for m in range(8):
                turned[k, pl.ds(m, 16, stride=8), :] = totals[pl.ds((c * CHUNK + k) * BLOCK + m * 16, 16), :]
        both = []
        for k, span in enumerate(spans):
            average = (turned[k] / divisor[span, :]).astype(jnp.bfloat16)
            own = table[mine + c * CHUNK + k]
            both.append(jnp.concatenate([own, average], axis=1))
        weights = jnp.concatenate([w_self[...], w_neigh[...]], axis=0)
        for span, lhs in zip(spans, both):
            hidden = jnp.dot(lhs, weights, preferred_element_type=jnp.float32) + bias[...]
            out[span, :] = jnp.maximum(hidden, 0.0).astype(jnp.bfloat16)
        out_copy(c).start()

    for c in range(CHUNKS):
        out_copy(c).wait()


def layer(plan, words, table, before, divisor, w_self, w_neigh, bias):
    vmem = pl.BlockSpec(memory_space=pltpu.VMEM)
    smem = pl.BlockSpec(memory_space=pltpu.SMEM)
    hbm = pl.BlockSpec(memory_space=pl.ANY)
    plan = pltpu.with_memory_space_constraint(plan, pltpu.SMEM)
    words, table, before, divisor = (
        pltpu.with_memory_space_constraint(a, pltpu.VMEM) for a in (words, table, before, divisor)
    )
    return pl.pallas_call(
        layer_kernel,
        out_shape=jax.ShapeDtypeStruct((ROWS, 512), jnp.bfloat16),
        in_specs=[smem] + [vmem] * 7,
        out_specs=hbm,
        scratch_shapes=[
            pltpu.SMEM((RB * 10 + FAN,), jnp.int32),
            pltpu.VMEM((ROWS, BLOCK), jnp.float32),
            pltpu.VMEM((ROWS, 512), jnp.bfloat16),
            pltpu.VMEM((CHUNK, BLOCK, BLOCK), jnp.float32),
            pltpu.SemaphoreType.DMA((CHUNKS,)),
        ],
        compiler_params=pltpu.CompilerParams(vmem_limit_bytes=20 * 2**20),
        name="layer",
    )(plan, words, table, before, divisor, w_self, w_neigh, bias.reshape(1, 512))


def on_device(
    x_current, x_cached, w_self, w_neigh, bias, tile_columns, tile_count, adjacency, degree, boundary_blocks
):
    words = adjacency.reshape(RB, 5, 8, 16, BLOCK).transpose(0, 1, 3, 2, 4).reshape(RB * WORDS, BLOCK)
    gathered = gather(
        tile_columns, tile_count, boundary_blocks, degree.reshape(SIDE, 8, BLOCK), x_current.reshape(RB, BLOCK, BLOCK), x_cached.reshape(RB, BLOCK, BLOCK), words
    )
    return layer(*gathered, w_self, w_neigh, bias)


def solution(mesh):
    rows = P(("dom", "grp"), None)
    line = P(("dom", "grp"))
    return jax.shard_map(
        on_device,
        mesh=mesh,
        in_specs=(rows, rows, P(), P(), P(), rows, line, P(("dom", "grp"), None, None), line, rows),
        out_specs=rows,
        check_vma=False,
    )
```

```python
import jax
import jax.numpy as jnp
from jax import lax
from jax.experimental import pallas as pl
from jax.experimental.pallas import tpu as pltpu
from jax.sharding import PartitionSpec as P

MESH = pl.DeviceIdType.MESH
SIDE = 4
BLOCK = 128
RB = 32
SLOTS = 40
WORDS = 640
ROWS = RB * BLOCK
SOON = 8
NEXT = 4
HALO = 20
REST = 64
WHO, LEFT = 126, 127
FAN = 16
CHUNK = 4
CHUNKS = RB // CHUNK


def sort_slots(cols, counts, me, wide, live):
    wide[...] = jnp.zeros_like(wide)
    wide[:, :SLOTS] = cols[...]
    for r in range(RB):
        live[pl.ds(r, 1), :] = jnp.full((1, BLOCK), counts[r], jnp.int32)
    c = wide[...]
    t = lax.broadcasted_iota(jnp.int32, (RB, BLOCK), 1)
    on = t < live[...]
    d, b = ((c >> 5) - me) & 3, c & 31
    soon = (d == 0) | ((d == 3) & (b < 16)) | ((d == 1) & (b >= 16))
    e = c - 128
    y, core, z, x = e & 3, (e >> 2) & 1, (e >> 3) & 3, (e >> 5) & 3
    place = core * 64 + (y >> 1) * 32 + jnp.where(y < 2, z * 4 + x, x * 4 + z) * 2 + (y & 1)
    inside = c < 128
    kind = jnp.where(inside, jnp.where(soon, 0, jnp.where(d == 2, 3, 1)), 2)
    both = jnp.where(on, kind, 4) << 22
    near_place = jnp.where(d == 0, b, jnp.where(soon, 32 + b, jnp.where(d == 3, b & 15, 16 + (b & 15))))
    index = (jnp.where(inside, near_place, place) << 6) | (jnp.where(inside, c, 128 + place) << 13)
    both = both | t | index | (1 << 21)
    table = jnp.zeros((RB, BLOCK), jnp.int32)
    soons = nexts = halos = rests = jnp.zeros((RB, BLOCK), jnp.int32)
    for s in range(SLOTS):
        one = jnp.broadcast_to(both[:, s : s + 1], (RB, BLOCK))
        kind = one >> 22
        soon = (kind == 0) & (soons < SOON)
        after = (kind == 1) & (nexts < NEXT)
        halo = (kind == 2) & (halos < HALO)
        rest = (kind < 4) & jnp.logical_not(soon | after | halo)
        target = jnp.where(halo, SOON + NEXT + halos, jnp.where(rest, REST + rests, -1))
        target = jnp.where(soon, soons, jnp.where(after, SOON + nexts, target))
        table = jnp.where(target == t, one & ((1 << 22) - 1), table)
        soons += jnp.where(soon, 1, 0)
        nexts += jnp.where(after, 1, 0)
        halos += jnp.where(halo, 1, 0)
        rests += jnp.where(rest, 1, 0)
    table = jnp.where(t == LEFT, rests, jnp.where(t == WHO, me, table))
    return table


class Unpack:
    def __init__(self):
        lane = lax.broadcasted_iota(jnp.int32, (16, BLOCK), 1)
        self.source = lane >> 3
        bit = lane & 7
        self.low_bit = (1 << bit).astype(jnp.int16)
        self.high_bit = jnp.where(bit == 7, -32768, 1 << (bit + 8)).astype(jnp.int16)

    def four(self, words, rows, keeps):
        one = jnp.ones((16, BLOCK), jnp.bfloat16)
        zero = jnp.zeros((16, BLOCK), jnp.bfloat16)
        packed = None
        for k, (row, keep) in enumerate(zip(rows, keeps)):
            mask = keep & (255 << (8 * k) if k < 3 else -16777216)
            word = (words[row] << (8 * k)) & mask
            packed = word if packed is None else packed | word
        tiles = [[], [], [], []]
        for m in range(8):
            spread = jnp.take_along_axis(packed, self.source + 16 * m, axis=1, mode="promise_in_bounds")
            low = spread.astype(jnp.int16)
            high = (spread >> 16).astype(jnp.int16)
            for tile, half, mask in zip(tiles, (low, low, high, high), (self.low_bit, self.high_bit) * 2):
                tile.append(jnp.where((half & mask) != 0, one, zero))
        return [jnp.concatenate(tile, axis=0) for tile in tiles]


def sum_tiles(unpack, plan, r, first, count, words, table, shift, blocks):
    tiles, features = [], []
    for group in range(count // 4):
        entries = [plan[r, first + group * 4 + k] for k in range(4)]
        rows = [r * SLOTS + (e & 63) for e in entries]
        tiles += unpack.four(words, rows, [-(e >> 21) for e in entries])
        for e in entries:
            block = (e >> shift) & (blocks - 1)
            features.append(table[block])
    return jnp.dot(
        jnp.concatenate(tiles, axis=1), jnp.concatenate(features, axis=0), preferred_element_type=jnp.float32
    )


def gather_kernel(
    cols_hbm, counts_hbm, exported, degree_hbm, xcur, cached_hbm, words_hbm,
    plan, words, table, totals, divisor,
    cols, counts, degree, wide, live, cached, raw, soon, after, halo, local_sem, send_sem, recv_sem,
):
    dom = lax.axis_index("dom")
    y = lax.axis_index("grp")
    core = dom % 2
    z = (dom // 2) % SIDE
    x = dom // (2 * SIDE)

    def at(xx, zz, cc, yy):
        return ((xx * SIDE + zz) * 2 + cc, yy)

    up, down, far = (y + 1) % SIDE, (y + 3) % SIDE, (y + 2) % SIDE
    y_up, y_down, y_far = at(x, z, core, up), at(x, z, core, down), at(x, z, core, far)
    x_others = [at((x + k) % SIDE, z, core, y) for k in (3, 1, 2)]
    z_others = [at(x, (z + k) % SIDE, core, y) for k in (3, 1, 2)]
    sibling = at(x, z, 1 - core, y)
    cached_copy = pltpu.make_async_copy(cached_hbm, cached, local_sem.at[0])
    cached_copy.start()
    words_copy = pltpu.make_async_copy(words_hbm, raw, local_sem.at[2])
    words_copy.start()
    small_copies = [
        pltpu.make_async_copy(src, dst, local_sem.at[7 + k])
        for k, (src, dst) in enumerate(
            ((cols_hbm, cols), (counts_hbm, counts), (degree_hbm, degree))
        )
    ]
    for copy in small_copies:
        copy.start()
    peers = [y_up, y_down, y_far, *x_others, *z_others, sibling]
    barrier = pltpu.get_barrier_semaphore()
    for peer in peers:
        pl.semaphore_signal(barrier, inc=1, device_id=peer, device_id_type=MESH)
    pl.semaphore_wait(barrier, len(peers))

    started = []

    def send(src, dst, sem, to):
        copy = pltpu.make_async_remote_copy(
            src_ref=src,
            dst_ref=dst,
            send_sem=send_sem.at[sem],
            recv_sem=recv_sem.at[sem],
            device_id=to,
            device_id_type=MESH,
        )
        copy.start()
        started.append(copy)

    def landed(dst, sem):
        pltpu.make_async_remote_copy(
            src_ref=dst,
            dst_ref=dst,
            send_sem=send_sem.at[sem],
            recv_sem=recv_sem.at[sem],
            device_id=sibling,
            device_id_type=MESH,
        ).wait_recv()

    def blocks(first, count):
        return halo.at[pl.ds(first, count)]

    part_half = RB // 2
    halves = pl.ds(0, part_half), pl.ds(part_half, part_half)
    from_down, from_up = soon.at[pl.ds(RB, part_half)], soon.at[pl.ds(RB + part_half, part_half)]

    def far_rows(first):
        return table.at[pl.ds(first, RB // 2)]

    base = core * 64

    def place(yy):
        ring = jnp.where(yy < 2, z * SIDE + x, x * SIDE + z)
        return base + (yy // 2) * 32 + ring * 2 + yy % 2

    own = blocks(place(y), 1)
    cached_copy.wait()
    for copy in small_copies:
        copy.wait()
    chosen = cached[exported[0, 0]]
    halo[place(y)] = chosen
    for sem, peer in enumerate((y_up, y_down, y_far)):
        send(own, own, sem, peer)
    send(xcur.at[halves[0]], from_down, 3, y_up)
    send(xcur.at[halves[1]], from_up, 4, y_down)
    part_copy = pltpu.make_async_copy(xcur, soon.at[pl.ds(0, RB)], local_sem.at[1])
    part_copy.start()
    wide[...] = sort_slots(cols, counts, y, wide, live)
    plan_copy = pltpu.make_async_copy(wide, plan, local_sem.at[0])
    plan_copy.start()
    landed(blocks(place(down), 1), 0)
    landed(blocks(place(up), 1), 1)
    landed(blocks(place(far), 1), 2)

    first = [
        (lambda m: base + (z * SIDE + m) * 2, x, x_others),
        (lambda m: base + 32 + (x * SIDE + m) * 2, z, z_others),
    ]
    second = [
        (lambda m: base + m * 8, z, z_others),
        (lambda m: base + 32 + m * 8, x, x_others),
    ]
    for half, (piece, me, others) in enumerate(first):
        for k, other in enumerate(others):
            send(blocks(piece(me), 2), blocks(piece(me), 2), 8 + 4 * half + k, other)

    words_copy.wait()

    @pl.loop(0, RB)
    def _(r):
        for t in range(SLOTS):
            slot = raw[pl.ds(r * WORDS + (t // 8) * BLOCK + t % 8, 16, stride=8), :]
            words[r * SLOTS + t] = slot

    send(xcur.at[halves[1]], after.at[halves[0]], 32, y_up)
    send(xcur.at[halves[0]], after.at[halves[1]], 33, y_down)

    for half, (piece, me, _) in enumerate(first):
        for k, d in enumerate((1, 3, 2)):
            landed(blocks(piece((me + d) % SIDE), 2), 8 + 4 * half + k)
        piece2, me2, others2 = second[half]
        mine = blocks(piece2(me2), 8)
        for k in (2, 0, 1):
            send(mine, mine, 16 + 4 * half + k, others2[k])
        send(mine, mine, 24 + 4 * half, sibling)

    @pl.loop(0, RB)
    def _(r):
        row = degree[r // 8, pl.ds(r % 8, 1), :].astype(jnp.float32)
        divisor[pl.ds(pl.multiple_of(r * BLOCK, BLOCK), BLOCK), :] = jnp.broadcast_to(row, (BLOCK, BLOCK)).T

    def pass_on(k, d):
        for half, (piece, me, _) in enumerate(second):
            got = blocks(piece((me + d) % SIDE), 8)
            landed(got, 16 + 4 * half + k)
            send(got, got, 25 + 4 * half + k, sibling)

    part_copy.wait()
    plan_copy.wait()
    landed(from_down, 3)
    landed(from_up, 4)
    unpack = Unpack()

    def add_tiles(first, count, source, each, start=False):
        @pl.loop(0, RB // each)
        def _(step):
            for k in range(each):
                r = step * each + k
                value = sum_tiles(unpack, plan, r, first, count, words, source, 6, source.shape[0])
                span = pl.ds(pl.multiple_of(r * BLOCK, BLOCK), BLOCK)
                totals[span, :] = value if start else totals[span, :] + value

    send(from_down, far_rows(down * RB), 5, y_up)
    send(from_up, far_rows(up * RB + part_half), 6, y_down)
    add_tiles(0, SOON, soon, 8, start=True)

    def keep(k, src, first):
        copy = pltpu.make_async_copy(src, table.at[pl.ds(first, src.shape[0])], local_sem.at[k])
        copy.start()
        return copy

    pass_on(0, 1)
    pass_on(1, 3)
    pass_on(2, 2)
    landed(after.at[halves[0]], 32)
    landed(after.at[halves[1]], 33)
    kept = [
        keep(3, soon.at[pl.ds(0, RB)], y * RB),
        keep(4, from_down, down * RB),
        keep(5, from_up, up * RB + part_half),
        keep(6, after.at[halves[0]], down * RB + part_half),
        keep(0, after.at[halves[1]], up * RB),
    ]
    add_tiles(SOON, NEXT, after, 8)

    other = (1 - core) * 64
    for half, (start, me) in enumerate(((other, z), (other + 32, x))):
        for k, d in enumerate((0, 1, 3, 2)):
            landed(blocks(start + (me + d) % SIDE * 8, 8), 24 + 4 * half + k)
    kept.append(keep(1, halo, SIDE * RB))
    add_tiles(SOON + NEXT, HALO, halo, 4)
    for copy in kept:
        copy.wait()
    landed(far_rows(far * RB), 5)
    landed(far_rows(far * RB + part_half), 6)
    for copy in started:
        copy.wait_send()


def gather(cols, counts, exported, degree, xcur, cached, words):
    hbm = pl.BlockSpec(memory_space=pl.ANY)
    vmem = pl.BlockSpec(memory_space=pltpu.VMEM)
    smem = pl.BlockSpec(memory_space=pltpu.SMEM)
    operands = [
        pltpu.with_memory_space_constraint(a, pltpu.HBM) for a in (cols, counts, degree, xcur, cached, words)
    ]
    operands.insert(2, exported)
    return pl.pallas_call(
        gather_kernel,
        out_shape=(
            pltpu.SMEM((RB, BLOCK), jnp.int32),
            pltpu.VMEM((RB * SLOTS, 16, BLOCK), jnp.int32),
            pltpu.VMEM((256, BLOCK, BLOCK), jnp.bfloat16),
            pltpu.VMEM((ROWS, BLOCK), jnp.float32),
            pltpu.VMEM((ROWS, BLOCK), jnp.float32),
        ),
        in_specs=[hbm, hbm, smem, hbm, hbm, hbm, hbm],
        out_specs=(smem, vmem, vmem, vmem, vmem),
        scratch_shapes=[
            pltpu.VMEM((RB, SLOTS), jnp.int32),
            pltpu.SMEM((RB,), jnp.int32),
            pltpu.VMEM((SIDE, 8, BLOCK), jnp.int32),
            pltpu.VMEM((RB, BLOCK), jnp.int32),
            pltpu.VMEM((RB, BLOCK), jnp.int32),
            pltpu.VMEM((RB, BLOCK, BLOCK), jnp.bfloat16),
            pltpu.VMEM((RB * WORDS, BLOCK), jnp.int32),
            pltpu.VMEM((2 * RB, BLOCK, BLOCK), jnp.bfloat16),
            pltpu.VMEM((RB, BLOCK, BLOCK), jnp.bfloat16),
            pltpu.VMEM((128, BLOCK, BLOCK), jnp.bfloat16),
            pltpu.SemaphoreType.DMA((11,)),
            pltpu.SemaphoreType.DMA((34,)),
            pltpu.SemaphoreType.DMA((34,)),
        ],
        compiler_params=pltpu.CompilerParams(
            collective_id=0, has_side_effects=True, vmem_limit_bytes=26 * 2**20
        ),
        name="gather",
    )(*operands)


def layer_kernel(
    plan, words, table, before, divisor, w_self, w_neigh, bias, out_hbm, groups, totals, out, turned, out_sem
):
    def out_copy(c):
        span = pl.ds(pl.multiple_of(c * CHUNK * BLOCK, BLOCK), CHUNK * BLOCK)
        return pltpu.make_async_copy(out.at[span], out_hbm.at[span], out_sem.at[c])

    def list_groups(r, at):
        def one(q, at):
            groups[at] = r * 16 + q
            return at + 1

        return lax.fori_loop(0, (plan[r, LEFT] + 3) // 4, one, at)

    total = lax.fori_loop(0, RB, list_groups, 0)
    for k in range(FAN):
        groups[total + k] = -1
    totals[...] = before[...]
    unpack = Unpack()

    def product(at):
        code = groups[at]
        live = code >= 0
        code = jnp.maximum(code, 0)
        r = code >> 4
        first = jnp.where(live, REST + (code & 15) * 4, BLOCK - 8)
        return r, sum_tiles(unpack, plan, r, first, 4, words, table, 13, 256)

    @pl.loop(0, (total + FAN - 1) // FAN)
    def _(step):
        for r, value in [product(step * FAN + k) for k in range(FAN)]:
            totals[pl.ds(pl.multiple_of(r * BLOCK, BLOCK), BLOCK), :] += value

    mine = plan[0, WHO] * RB

    @pl.loop(0, CHUNKS)
    def _(c):
        spans = [pl.ds(pl.multiple_of((c * CHUNK + k) * BLOCK, BLOCK), BLOCK) for k in range(CHUNK)]
        for k in range(CHUNK):
            for m in range(8):
                turned[k, pl.ds(m, 16, stride=8), :] = totals[pl.ds((c * CHUNK + k) * BLOCK + m * 16, 16), :]
        both = []
        for k, span in enumerate(spans):
            average = (turned[k] / divisor[span, :]).astype(jnp.bfloat16)
            own = table[mine + c * CHUNK + k]
            both.append(jnp.concatenate([own, average], axis=1))
        weights = jnp.concatenate([w_self[...], w_neigh[...]], axis=0)
        for span, lhs in zip(spans, both):
            hidden = jnp.dot(lhs, weights, preferred_element_type=jnp.float32) + bias[...]
            out[span, :] = jnp.maximum(hidden, 0.0).astype(jnp.bfloat16)
        out_copy(c).start()

    for c in range(CHUNKS):
        out_copy(c).wait()


def layer(plan, words, table, before, divisor, w_self, w_neigh, bias):
    vmem = pl.BlockSpec(memory_space=pltpu.VMEM)
    smem = pl.BlockSpec(memory_space=pltpu.SMEM)
    hbm = pl.BlockSpec(memory_space=pl.ANY)
    plan = pltpu.with_memory_space_constraint(plan, pltpu.SMEM)
    words, table, before, divisor = (
        pltpu.with_memory_space_constraint(a, pltpu.VMEM) for a in (words, table, before, divisor)
    )
    return pl.pallas_call(
        layer_kernel,
        out_shape=jax.ShapeDtypeStruct((ROWS, 512), jnp.bfloat16),
        in_specs=[smem] + [vmem] * 7,
        out_specs=hbm,
        scratch_shapes=[
            pltpu.SMEM((RB * 10 + FAN,), jnp.int32),
            pltpu.VMEM((ROWS, BLOCK), jnp.float32),
            pltpu.VMEM((ROWS, 512), jnp.bfloat16),
            pltpu.VMEM((CHUNK, BLOCK, BLOCK), jnp.float32),
            pltpu.SemaphoreType.DMA((CHUNKS,)),
        ],
        compiler_params=pltpu.CompilerParams(vmem_limit_bytes=20 * 2**20),
        name="layer",
    )(plan, words, table, before, divisor, w_self, w_neigh, bias.reshape(1, 512))


def on_device(
    x_current, x_cached, w_self, w_neigh, bias, tile_columns, tile_count, adjacency, degree, boundary_blocks
):
    words = adjacency.reshape(RB, 5, 8, 16, BLOCK).transpose(0, 1, 3, 2, 4).reshape(RB * WORDS, BLOCK)
    gathered = gather(
        tile_columns, tile_count, boundary_blocks, degree.reshape(SIDE, 8, BLOCK), x_current.reshape(RB, BLOCK, BLOCK), x_cached.reshape(RB, BLOCK, BLOCK), words
    )
    return layer(*gathered, w_self, w_neigh, bias)


def solution(mesh):
    rows = P(("dom", "grp"), None)
    line = P(("dom", "grp"))
    return jax.shard_map(
        on_device,
        mesh=mesh,
        in_specs=(rows, rows, P(), P(), P(), rows, line, P(("dom", "grp"), None, None), line, rows),
        out_specs=rows,
        check_vma=False,
    )
```

```python
import jax
import jax.numpy as jnp
from jax import lax
from jax.experimental import pallas as pl
from jax.experimental.pallas import tpu as pltpu
from jax.sharding import PartitionSpec as P

MESH = pl.DeviceIdType.MESH
SIDE = 4
BLOCK = 128
RB = 32
SLOTS = 40
WORDS = 640
ROWS = RB * BLOCK
SOON = 8
NEXT = 4
HALO = 20
REST = 64
WHO, LEFT = 126, 127
FAN = 16
CHUNK = 8
CHUNKS = RB // CHUNK


def sort_slots(cols, counts, me, wide, live):
    wide[...] = jnp.zeros_like(wide)
    wide[:, :SLOTS] = cols[...]
    for r in range(RB):
        live[pl.ds(r, 1), :] = jnp.full((1, BLOCK), counts[r], jnp.int32)
    c = wide[...]
    t = lax.broadcasted_iota(jnp.int32, (RB, BLOCK), 1)
    on = t < live[...]
    d, b = ((c >> 5) - me) & 3, c & 31
    soon = (d == 0) | ((d == 3) & (b < 16)) | ((d == 1) & (b >= 16))
    e = c - 128
    y, core, z, x = e & 3, (e >> 2) & 1, (e >> 3) & 3, (e >> 5) & 3
    place = core * 64 + (y >> 1) * 32 + jnp.where(y < 2, z * 4 + x, x * 4 + z) * 2 + (y & 1)
    inside = c < 128
    kind = jnp.where(inside, jnp.where(soon, 0, jnp.where(d == 2, 3, 1)), 2)
    both = jnp.where(on, kind, 4) << 22
    near_place = jnp.where(d == 0, b, jnp.where(soon, 32 + b, jnp.where(d == 3, b & 15, 16 + (b & 15))))
    index = (jnp.where(inside, near_place, place) << 6) | (jnp.where(inside, c, 128 + place) << 13)
    both = both | t | index | (1 << 21)
    table = jnp.zeros((RB, BLOCK), jnp.int32)
    soons = nexts = halos = rests = jnp.zeros((RB, BLOCK), jnp.int32)
    for s in range(SLOTS):
        one = jnp.broadcast_to(both[:, s : s + 1], (RB, BLOCK))
        kind = one >> 22
        soon = (kind == 0) & (soons < SOON)
        after = (kind == 1) & (nexts < NEXT)
        halo = (kind == 2) & (halos < HALO)
        rest = (kind < 4) & jnp.logical_not(soon | after | halo)
        target = jnp.where(halo, SOON + NEXT + halos, jnp.where(rest, REST + rests, -1))
        target = jnp.where(soon, soons, jnp.where(after, SOON + nexts, target))
        table = jnp.where(target == t, one & ((1 << 22) - 1), table)
        soons += jnp.where(soon, 1, 0)
        nexts += jnp.where(after, 1, 0)
        halos += jnp.where(halo, 1, 0)
        rests += jnp.where(rest, 1, 0)
    table = jnp.where(t == LEFT, rests, jnp.where(t == WHO, me, table))
    return table


class Unpack:
    def __init__(self):
        lane = lax.broadcasted_iota(jnp.int32, (16, BLOCK), 1)
        self.source = lane >> 3
        bit = lane & 7
        self.low_bit = (1 << bit).astype(jnp.int16)
        self.high_bit = jnp.where(bit == 7, -32768, 1 << (bit + 8)).astype(jnp.int16)

    def four(self, words, rows, keeps):
        one = jnp.ones((16, BLOCK), jnp.bfloat16)
        zero = jnp.zeros((16, BLOCK), jnp.bfloat16)
        packed = None
        for k, (row, keep) in enumerate(zip(rows, keeps)):
            mask = keep & (255 << (8 * k) if k < 3 else -16777216)
            word = (words[row] << (8 * k)) & mask
            packed = word if packed is None else packed | word
        tiles = [[], [], [], []]
        for m in range(8):
            spread = jnp.take_along_axis(packed, self.source + 16 * m, axis=1, mode="promise_in_bounds")
            low = spread.astype(jnp.int16)
            high = (spread >> 16).astype(jnp.int16)
            for tile, half, mask in zip(tiles, (low, low, high, high), (self.low_bit, self.high_bit) * 2):
                tile.append(jnp.where((half & mask) != 0, one, zero))
        return [jnp.concatenate(tile, axis=0) for tile in tiles]


def sum_tiles(unpack, plan, r, first, count, words, table, shift, blocks):
    tiles, features = [], []
    for group in range(count // 4):
        entries = [plan[r, first + group * 4 + k] for k in range(4)]
        rows = [r * SLOTS + (e & 63) for e in entries]
        tiles += unpack.four(words, rows, [-(e >> 21) for e in entries])
        for e in entries:
            block = (e >> shift) & (blocks - 1)
            features.append(table[block])
    return jnp.dot(
        jnp.concatenate(tiles, axis=1), jnp.concatenate(features, axis=0), preferred_element_type=jnp.float32
    )


def gather_kernel(
    cols_hbm, counts_hbm, exported, degree_hbm, xcur, cached_hbm, words_hbm,
    plan, words, table, totals, divisor,
    cols, counts, degree, wide, live, cached, raw, soon, after, halo, local_sem, send_sem, recv_sem,
):
    dom = lax.axis_index("dom")
    y = lax.axis_index("grp")
    core = dom % 2
    z = (dom // 2) % SIDE
    x = dom // (2 * SIDE)

    def at(xx, zz, cc, yy):
        return ((xx * SIDE + zz) * 2 + cc, yy)

    up, down, far = (y + 1) % SIDE, (y + 3) % SIDE, (y + 2) % SIDE
    y_up, y_down, y_far = at(x, z, core, up), at(x, z, core, down), at(x, z, core, far)
    x_others = [at((x + k) % SIDE, z, core, y) for k in (3, 1, 2)]
    z_others = [at(x, (z + k) % SIDE, core, y) for k in (3, 1, 2)]
    sibling = at(x, z, 1 - core, y)
    cached_copy = pltpu.make_async_copy(cached_hbm, cached, local_sem.at[0])
    cached_copy.start()
    words_copy = pltpu.make_async_copy(words_hbm, raw, local_sem.at[2])
    words_copy.start()
    small_copies = [
        pltpu.make_async_copy(src, dst, local_sem.at[7 + k])
        for k, (src, dst) in enumerate(
            ((cols_hbm, cols), (counts_hbm, counts), (degree_hbm, degree))
        )
    ]
    for copy in small_copies:
        copy.start()
    peers = [y_up, y_down, y_far, *x_others, *z_others, sibling]
    barrier = pltpu.get_barrier_semaphore()
    for peer in peers:
        pl.semaphore_signal(barrier, inc=1, device_id=peer, device_id_type=MESH)
    pl.semaphore_wait(barrier, len(peers))

    started = []

    def send(src, dst, sem, to):
        copy = pltpu.make_async_remote_copy(
            src_ref=src,
            dst_ref=dst,
            send_sem=send_sem.at[sem],
            recv_sem=recv_sem.at[sem],
            device_id=to,
            device_id_type=MESH,
        )
        copy.start()
        started.append(copy)

    def landed(dst, sem):
        pltpu.make_async_remote_copy(
            src_ref=dst,
            dst_ref=dst,
            send_sem=send_sem.at[sem],
            recv_sem=recv_sem.at[sem],
            device_id=sibling,
            device_id_type=MESH,
        ).wait_recv()

    def blocks(first, count):
        return halo.at[pl.ds(first, count)]

    part_half = RB // 2
    halves = pl.ds(0, part_half), pl.ds(part_half, part_half)
    from_down, from_up = soon.at[pl.ds(RB, part_half)], soon.at[pl.ds(RB + part_half, part_half)]

    def far_rows(first):
        return table.at[pl.ds(first, RB // 2)]

    base = core * 64

    def place(yy):
        ring = jnp.where(yy < 2, z * SIDE + x, x * SIDE + z)
        return base + (yy // 2) * 32 + ring * 2 + yy % 2

    own = blocks(place(y), 1)
    cached_copy.wait()
    for copy in small_copies:
        copy.wait()
    chosen = cached[exported[0, 0]]
    halo[place(y)] = chosen
    for sem, peer in enumerate((y_up, y_down, y_far)):
        send(own, own, sem, peer)
    send(xcur.at[halves[0]], from_down, 3, y_up)
    send(xcur.at[halves[1]], from_up, 4, y_down)
    part_copy = pltpu.make_async_copy(xcur, soon.at[pl.ds(0, RB)], local_sem.at[1])
    part_copy.start()
    wide[...] = sort_slots(cols, counts, y, wide, live)
    plan_copy = pltpu.make_async_copy(wide, plan, local_sem.at[0])
    plan_copy.start()
    landed(blocks(place(down), 1), 0)
    landed(blocks(place(up), 1), 1)
    landed(blocks(place(far), 1), 2)

    first = [
        (lambda m: base + (z * SIDE + m) * 2, x, x_others),
        (lambda m: base + 32 + (x * SIDE + m) * 2, z, z_others),
    ]
    second = [
        (lambda m: base + m * 8, z, z_others),
        (lambda m: base + 32 + m * 8, x, x_others),
    ]
    for half, (piece, me, others) in enumerate(first):
        for k, other in enumerate(others):
            send(blocks(piece(me), 2), blocks(piece(me), 2), 8 + 4 * half + k, other)

    words_copy.wait()

    @pl.loop(0, RB)
    def _(r):
        for t in range(SLOTS):
            slot = raw[pl.ds(r * WORDS + (t // 8) * BLOCK + t % 8, 16, stride=8), :]
            words[r * SLOTS + t] = slot

    send(xcur.at[halves[1]], after.at[halves[0]], 32, y_up)
    send(xcur.at[halves[0]], after.at[halves[1]], 33, y_down)

    for half, (piece, me, _) in enumerate(first):
        for k, d in enumerate((1, 3, 2)):
            landed(blocks(piece((me + d) % SIDE), 2), 8 + 4 * half + k)
        piece2, me2, others2 = second[half]
        mine = blocks(piece2(me2), 8)
        for k in (2, 0, 1):
            send(mine, mine, 16 + 4 * half + k, others2[k])
        send(mine, mine, 24 + 4 * half, sibling)

    @pl.loop(0, RB)
    def _(r):
        row = degree[r // 8, pl.ds(r % 8, 1), :].astype(jnp.float32)
        divisor[pl.ds(pl.multiple_of(r * BLOCK, BLOCK), BLOCK), :] = jnp.broadcast_to(row, (BLOCK, BLOCK)).T

    def pass_on(k, d):
        for half, (piece, me, _) in enumerate(second):
            got = blocks(piece((me + d) % SIDE), 8)
            landed(got, 16 + 4 * half + k)
            send(got, got, 25 + 4 * half + k, sibling)

    part_copy.wait()
    plan_copy.wait()
    landed(from_down, 3)
    landed(from_up, 4)
    unpack = Unpack()

    def add_tiles(first, count, source, each, start=False):
        @pl.loop(0, RB // each)
        def _(step):
            for k in range(each):
                r = step * each + k
                value = sum_tiles(unpack, plan, r, first, count, words, source, 6, source.shape[0])
                span = pl.ds(pl.multiple_of(r * BLOCK, BLOCK), BLOCK)
                totals[span, :] = value if start else totals[span, :] + value

    send(from_down, far_rows(down * RB), 5, y_up)
    send(from_up, far_rows(up * RB + part_half), 6, y_down)
    add_tiles(0, SOON, soon, 8, start=True)

    def keep(k, src, first):
        copy = pltpu.make_async_copy(src, table.at[pl.ds(first, src.shape[0])], local_sem.at[k])
        copy.start()
        return copy

    pass_on(0, 1)
    pass_on(1, 3)
    pass_on(2, 2)
    landed(after.at[halves[0]], 32)
    landed(after.at[halves[1]], 33)
    kept = [
        keep(3, soon.at[pl.ds(0, RB)], y * RB),
        keep(4, from_down, down * RB),
        keep(5, from_up, up * RB + part_half),
        keep(6, after.at[halves[0]], down * RB + part_half),
        keep(0, after.at[halves[1]], up * RB),
    ]
    add_tiles(SOON, NEXT, after, 8)

    other = (1 - core) * 64
    for half, (start, me) in enumerate(((other, z), (other + 32, x))):
        for k, d in enumerate((0, 1, 3, 2)):
            landed(blocks(start + (me + d) % SIDE * 8, 8), 24 + 4 * half + k)
    kept.append(keep(1, halo, SIDE * RB))
    add_tiles(SOON + NEXT, HALO, halo, 4)
    for copy in kept:
        copy.wait()
    landed(far_rows(far * RB), 5)
    landed(far_rows(far * RB + part_half), 6)
    for copy in started:
        copy.wait_send()


def gather(cols, counts, exported, degree, xcur, cached, words):
    hbm = pl.BlockSpec(memory_space=pl.ANY)
    vmem = pl.BlockSpec(memory_space=pltpu.VMEM)
    smem = pl.BlockSpec(memory_space=pltpu.SMEM)
    operands = [
        pltpu.with_memory_space_constraint(a, pltpu.HBM) for a in (cols, counts, degree, xcur, cached, words)
    ]
    operands.insert(2, exported)
    return pl.pallas_call(
        gather_kernel,
        out_shape=(
            pltpu.SMEM((RB, BLOCK), jnp.int32),
            pltpu.VMEM((RB * SLOTS, 16, BLOCK), jnp.int32),
            pltpu.VMEM((256, BLOCK, BLOCK), jnp.bfloat16),
            pltpu.VMEM((ROWS, BLOCK), jnp.float32),
            pltpu.VMEM((ROWS, BLOCK), jnp.float32),
        ),
        in_specs=[hbm, hbm, smem, hbm, hbm, hbm, hbm],
        out_specs=(smem, vmem, vmem, vmem, vmem),
        scratch_shapes=[
            pltpu.VMEM((RB, SLOTS), jnp.int32),
            pltpu.SMEM((RB,), jnp.int32),
            pltpu.VMEM((SIDE, 8, BLOCK), jnp.int32),
            pltpu.VMEM((RB, BLOCK), jnp.int32),
            pltpu.VMEM((RB, BLOCK), jnp.int32),
            pltpu.VMEM((RB, BLOCK, BLOCK), jnp.bfloat16),
            pltpu.VMEM((RB * WORDS, BLOCK), jnp.int32),
            pltpu.VMEM((2 * RB, BLOCK, BLOCK), jnp.bfloat16),
            pltpu.VMEM((RB, BLOCK, BLOCK), jnp.bfloat16),
            pltpu.VMEM((128, BLOCK, BLOCK), jnp.bfloat16),
            pltpu.SemaphoreType.DMA((11,)),
            pltpu.SemaphoreType.DMA((34,)),
            pltpu.SemaphoreType.DMA((34,)),
        ],
        compiler_params=pltpu.CompilerParams(
            collective_id=0, has_side_effects=True, vmem_limit_bytes=26 * 2**20
        ),
        name="gather",
    )(*operands)


def layer_kernel(
    plan, words, table, before, divisor, w_self, w_neigh, bias, out_hbm, groups, totals, out, turned, out_sem
):
    def out_copy(c):
        span = pl.ds(pl.multiple_of(c * CHUNK * BLOCK, BLOCK), CHUNK * BLOCK)
        return pltpu.make_async_copy(out.at[span], out_hbm.at[span], out_sem.at[c])

    def list_groups(r, at):
        def one(q, at):
            groups[at] = r * 16 + q
            return at + 1

        return lax.fori_loop(0, (plan[r, LEFT] + 3) // 4, one, at)

    total = lax.fori_loop(0, RB, list_groups, 0)
    for k in range(FAN):
        groups[total + k] = -1
    totals[...] = before[...]
    unpack = Unpack()

    def product(at):
        code = groups[at]
        live = code >= 0
        code = jnp.maximum(code, 0)
        r = code >> 4
        first = jnp.where(live, REST + (code & 15) * 4, BLOCK - 8)
        return r, sum_tiles(unpack, plan, r, first, 4, words, table, 13, 256)

    @pl.loop(0, (total + FAN - 1) // FAN)
    def _(step):
        for r, value in [product(step * FAN + k) for k in range(FAN)]:
            totals[pl.ds(pl.multiple_of(r * BLOCK, BLOCK), BLOCK), :] += value

    mine = plan[0, WHO] * RB

    @pl.loop(0, CHUNKS)
    def _(c):
        spans = [pl.ds(pl.multiple_of((c * CHUNK + k) * BLOCK, BLOCK), BLOCK) for k in range(CHUNK)]
        for k in range(CHUNK):
            for m in range(8):
                turned[k, pl.ds(m, 16, stride=8), :] = totals[pl.ds((c * CHUNK + k) * BLOCK + m * 16, 16), :]
        both = []
        for k, span in enumerate(spans):
            average = (turned[k] / divisor[span, :]).astype(jnp.bfloat16)
            own = table[mine + c * CHUNK + k]
            both.append(jnp.concatenate([own, average], axis=1))
        weights = jnp.concatenate([w_self[...], w_neigh[...]], axis=0)
        for span, lhs in zip(spans, both):
            hidden = jnp.dot(lhs, weights, preferred_element_type=jnp.float32) + bias[...]
            out[span, :] = jnp.maximum(hidden, 0.0).astype(jnp.bfloat16)
        out_copy(c).start()

    for c in range(CHUNKS):
        out_copy(c).wait()


def layer(plan, words, table, before, divisor, w_self, w_neigh, bias):
    vmem = pl.BlockSpec(memory_space=pltpu.VMEM)
    smem = pl.BlockSpec(memory_space=pltpu.SMEM)
    hbm = pl.BlockSpec(memory_space=pl.ANY)
    plan = pltpu.with_memory_space_constraint(plan, pltpu.SMEM)
    words, table, before, divisor = (
        pltpu.with_memory_space_constraint(a, pltpu.VMEM) for a in (words, table, before, divisor)
    )
    return pl.pallas_call(
        layer_kernel,
        out_shape=jax.ShapeDtypeStruct((ROWS, 512), jnp.bfloat16),
        in_specs=[smem] + [vmem] * 7,
        out_specs=hbm,
        scratch_shapes=[
            pltpu.SMEM((RB * 10 + FAN,), jnp.int32),
            pltpu.VMEM((ROWS, BLOCK), jnp.float32),
            pltpu.VMEM((ROWS, 512), jnp.bfloat16),
            pltpu.VMEM((CHUNK, BLOCK, BLOCK), jnp.float32),
            pltpu.SemaphoreType.DMA((CHUNKS,)),
        ],
        compiler_params=pltpu.CompilerParams(vmem_limit_bytes=20 * 2**20),
        name="layer",
    )(plan, words, table, before, divisor, w_self, w_neigh, bias.reshape(1, 512))


def on_device(
    x_current, x_cached, w_self, w_neigh, bias, tile_columns, tile_count, adjacency, degree, boundary_blocks
):
    words = adjacency.reshape(RB, 5, 8, 16, BLOCK).transpose(0, 1, 3, 2, 4).reshape(RB * WORDS, BLOCK)
    gathered = gather(
        tile_columns, tile_count, boundary_blocks, degree.reshape(SIDE, 8, BLOCK), x_current.reshape(RB, BLOCK, BLOCK), x_cached.reshape(RB, BLOCK, BLOCK), words
    )
    return layer(*gathered, w_self, w_neigh, bias)


def solution(mesh):
    rows = P(("dom", "grp"), None)
    line = P(("dom", "grp"))
    return jax.shard_map(
        on_device,
        mesh=mesh,
        in_specs=(rows, rows, P(), P(), P(), rows, line, P(("dom", "grp"), None, None), line, rows),
        out_specs=rows,
        check_vma=False,
    )
```
